128 devices in a mesh: doc: 4 (over x), clu: 32 (over z, y, core).
Axes of the slice: x: 4, y: 4, z: 4, core: 2. Of those that a mesh axis runs over, the one named last changes fastest.
Arguments:
- embeddings: bfloat16 [16384, 4096], P(('doc', 'clu')), may hold values from -6 to 6
- cluster_ids: int32 [16384, 1], P(('doc', 'clu')), may hold values from 0 to 127; in each aligned block of 128 rows (0 to 127, 128 to 255, ...) at most 3 rows name the same one
Outputs:
- max_similarity: float32 [16384], P(('doc', 'clu'))
The draws below stay inside these ranges and needn't reach their ends.
Inputs may be any that keep to these rules, and one draw needn't show every extreme that they name: `cluster_ids`: within the 128 rows of one device no cluster id occurs more than 3 times, and in every draw some cluster occurs exactly 3 times among the rows of some device.
All inputs are finite; a program needn't handle non-finite values.
Results may differ from the reference program's by a relative error of at most 0.0016.
Values may be sent and summed in bfloat16 or wider, within the bound.
A program may use at most 64 MiB of HBM per device.

```python
import math
import jax
import jax.numpy as jnp
import numpy as np
from jax import lax

D = 4096
ROWS_DEV = 128
CLUSTERS = 128
CAP = 3
SLOTS = 384
ROWS = 16384


def levels(stream_key, extent, shards, least, top_value):
    def one(position, shards_of):
        steps = jax.random.uniform(jax.random.fold_in(jax.random.fold_in(stream_key, 6), position), (shards_of,), jnp.float32, least / len(shards), top_value / len(shards))
        return jnp.repeat(jnp.exp(steps), extent[position] // shards_of).reshape((-1,) + (1,) * (len(extent) - position - 1))

    gain = one(*shards[0])
    for cut in shards[1:]:
        gain = gain * one(*cut)
    return gain


def shared_out(stream_key, own, number, rows, count, top, most, lean):
    ranking = jax.random.permutation(stream_key, count)
    packed, common = load_shares(count, rows * top, most, lean, True), load_shares(count, rows * top, most, lean, False)
    places = jnp.arange(count)

    def named(tallies, offset_by):
        used = int((tallies > 0).sum())
        fixed = max(1, used // 4)
        shifted = fixed + (places - fixed + offset_by * (used - fixed)) % max(1, count - fixed)
        return jnp.zeros((count,), jnp.int32).at[ranking[jnp.where(places < fixed, places, shifted)]].set(jnp.asarray(tallies, jnp.int32))

    tallies = jnp.where(number % 4 == 0, named(packed, number // 4), named(common, number - number // 4 - 1))
    mixed = jax.random.permutation(jax.random.fold_in(own, 3), count)
    donor, sink = mixed[0:count // 2 * 2:2], mixed[1:count // 2 * 2:2]
    slack = jnp.minimum(tallies[donor] - 1, most - tallies[sink]) // 2
    slack = jnp.where((donor == ranking[0]) | (sink == ranking[0]) | (tallies[sink] == 0), 0, jnp.maximum(slack, 0))
    shifted = jax.random.randint(jax.random.fold_in(own, 4), (count // 2,), 0, 1 << 20) % (slack + 1)
    tallies = tallies.at[donor].add(-shifted).at[sink].add(shifted)
    items = jnp.searchsorted(jnp.cumsum(tallies), jnp.arange(rows * top), side="right").astype(jnp.int32)
    grid = items.reshape(top, rows).T
    grid = grid[jax.random.permutation(jax.random.fold_in(own, 1), rows)]
    offset_by = jax.random.randint(jax.random.fold_in(own, 2), (rows, 1), 0, top)
    return jnp.take_along_axis(grid, (jnp.arange(top)[None, :] + offset_by) % top, axis=1)


def load_shares(number_of, total, bound, lean, full):
    loads = [(1 << 20) // math.isqrt(rank ** lean) + 1 for rank in range(1, number_of + 1)]
    largest = bound if full else min(bound, max(-(-total // number_of), total * loads[0] // sum(loads)))
    least = 1 if total - largest >= number_of - 1 else 0
    given, rest = [largest] + [least] * (number_of - 1), total - largest - least * (number_of - 1)
    while rest > 0:
        candidates = [i for i in range(1, number_of) if given[i] < largest] or [i for i in range(1, number_of) if given[i] < bound]
        mass, remaining = sum([loads[i] for i in candidates]), rest
        for i in candidates:
            extra = min(bound - given[i], max(1, remaining * loads[i] // mass), rest)
            given[i] = given[i] + extra
            rest = rest - extra
    return np.array(given)


def scatter_about(own_key, dims, width, limit, split=(), kind=jnp.bfloat16):
    array = jax.random.normal(own_key, dims, jnp.float32) * width
    if len(split) > 0:
        array = levels(own_key, dims, split, -0.22, 0.18) * array
    return jnp.clip(array, min=-limit, max=limit).astype(kind)


def setup_inputs(seed: int = 0) -> dict:
    key_list = jax.random.split(jax.random.key(seed), 3)
    embeddings = scatter_about(key_list[0], (ROWS, D), 1.0, 6.0, ((0, 128),))
    cluster_ids_keys = jax.random.split(jax.random.fold_in(key_list[1], 1), ROWS // ROWS_DEV)
    cluster_ids_turns = jax.random.permutation(jax.random.fold_in(key_list[1], 3), ROWS // ROWS_DEV)
    cluster_ids = jax.vmap(lambda own, number: shared_out(jax.random.fold_in(key_list[1], 2), own, number, ROWS_DEV, CLUSTERS, 1, CAP, 2))(cluster_ids_keys, cluster_ids_turns).reshape((ROWS, 1))
    return {"embeddings": embeddings, "cluster_ids": cluster_ids}


def reference(embeddings, cluster_ids):
    values = embeddings.astype(jnp.float32)
    squares = lax.optimization_barrier(jnp.sum(values * values, axis=1, keepdims=True))
    normed = (values * lax.rsqrt(squares + 1e-06)).astype(jnp.bfloat16)
    cluster = cluster_ids[:, 0].astype(jnp.int32)
    total_rows = cluster.shape[0]
    ordering = jnp.argsort(cluster, stable=True).astype(jnp.int32)
    counts = lax.optimization_barrier(jnp.sum((cluster[:, None] == jnp.arange(CLUSTERS, dtype=jnp.int32)[None, :]).astype(jnp.int32), axis=0))
    offsets = jnp.cumsum(counts) - counts

    def per_cluster(which):
        places = jnp.arange(SLOTS, dtype=jnp.int32)
        filled = places < counts[which]
        positions = jnp.clip(offsets[which] + places, 0, total_rows - 1).astype(jnp.int32)
        members = ordering[positions]
        block_rows = normed[members]
        scores = jnp.einsum('id,jd->ij', block_rows.astype(jnp.float32), block_rows.astype(jnp.float32))
        row_iota = lax.broadcasted_iota(jnp.int32, (SLOTS, SLOTS), 0)
        col_iota = lax.broadcasted_iota(jnp.int32, (SLOTS, SLOTS), 1)
        allowed = filled[None, :] & (row_iota != col_iota)
        highest = lax.optimization_barrier(jnp.max(jnp.where(allowed, scores, jnp.float32(-1.0)), axis=1))
        target = jnp.where(filled, members, jnp.int32(total_rows)).astype(jnp.int32)
        return (highest, target)
    highest, target = lax.map(per_cluster, jnp.arange(CLUSTERS, dtype=jnp.int32))
    result = jnp.zeros((total_rows,), jnp.float32)
    return result.at[target.reshape(-1)].set(highest.reshape(-1), mode='drop')
```

```python
import functools

import jax
import jax.numpy as jnp
from jax import lax
from jax.experimental import pallas as pl
from jax.experimental.pallas import tpu as pltpu
from jax.sharding import PartitionSpec as P

MESH = pl.DeviceIdType.MESH
DEVICES = 128
ROWS = 128
CAP = 3
D = 4096
Q = 16
W = D // Q
GROUP = 16
GROUPS = DEVICES // GROUP
EMPTY = 8.0
EMPTY_SQUARES = 50.0 * D
STRIDE = 53
UNSTRIDE = pow(STRIDE, -1, DEVICES)


def position():
    doc, clu = lax.axis_index("doc"), lax.axis_index("clu")
    return doc, clu // 8, (clu // 2) % 4, clu % 2


def offsets(n):
    place = (STRIDE * (n + 1) + DEVICES - 1) % DEVICES
    core = 1 - place % 2
    x = 3 - (place // 2) % 4
    y = 3 - (place // 8) % 4
    z = 3 - place // 32
    return x, z, y, core


def device(x, z, y, core):
    return x % 4, (z % 4) * 8 + (y % 4) * 2 + core % 2


def target(me, n):
    return device(*(a + b for a, b in zip(me, offsets(n))))


def origin(me, n):
    return device(*(a + 4 - b for a, b in zip(me, offsets(n))))


def slot_of(cluster, me):
    x, z, y, core = me
    dx = (cluster // 32 + 4 - x) % 4
    dz = ((cluster // 8) % 4 + 4 - z) % 4
    dy = ((cluster // 2) % 4 + 4 - y) % 4
    dc = (cluster % 2 + 2 - core) % 2
    place = (((3 - dz) * 4 + (3 - dy)) * 4 + (3 - dx)) * 2 + (1 - dc)
    return (UNSTRIDE * (place + 1) + DEVICES - 1) % DEVICES


def kernel(
    ids_ref, emb_ref, out_ref,
    blocks, outgoing, incoming, members, gram, index_v, index_s, highest, returned,
    index_sem, send_sem, recv_sem, back_send_sem, back_recv_sem,
):
    me = position()
    barrier = pltpu.get_barrier_semaphore()

    @pl.loop(0, DEVICES - 1)
    def _(n):
        pl.semaphore_signal(barrier, inc=1, device_id=target(me, n), device_id_type=MESH)

    rows = lax.broadcasted_iota(jnp.int32, (ROWS, DEVICES), 0)
    lanes = lax.broadcasted_iota(jnp.int32, (ROWS, DEVICES), 1)
    named = slot_of(ids_ref[...], me) == lanes
    earlier = jnp.dot(
        (lanes < rows).astype(jnp.bfloat16), named.astype(jnp.bfloat16), preferred_element_type=jnp.float32
    )
    place = jnp.sum(jnp.where(named, earlier, 0.0), axis=1, keepdims=True)
    for p in range(CAP):
        here = named & (earlier == p)
        row = ROWS + jnp.sum(jnp.where(here, rows - ROWS, 0), axis=0, keepdims=True)
        index_v[p : p + 1, :] = jnp.clip(row, 0, ROWS)
    to_scalars = pltpu.make_async_copy(index_v, index_s, index_sem)
    to_scalars.start()

    a = lax.broadcasted_iota(jnp.int32, (GROUP * Q, GROUP * Q), 0)
    b = lax.broadcasted_iota(jnp.int32, (GROUP * Q, GROUP * Q), 1)
    swap = ((a // Q == b % GROUP) & (a % Q == b // GROUP)).astype(jnp.bfloat16)

    for g in range(ROWS // GROUP):
        group = pl.ds(g * GROUP, GROUP)
        parts = jnp.concatenate([emb_ref[group, q * W : (q + 1) * W] for q in range(Q)], axis=0)
        swapped = jnp.dot(swap, parts, preferred_element_type=jnp.float32).astype(jnp.bfloat16)
        blocks[group] = swapped.reshape(GROUP, Q, W)
    blocks[ROWS] = jnp.full((Q, W), EMPTY, jnp.bfloat16)

    to_scalars.wait()
    pl.semaphore_wait(barrier, DEVICES - 1)

    @pl.loop(0, DEVICES - 1)
    def _(n):
        for p in range(CAP):
            outgoing[n, p] = blocks[index_s[p, n]]
        pltpu.make_async_remote_copy(
            src_ref=outgoing.at[n],
            dst_ref=incoming.at[n],
            send_sem=send_sem,
            recv_sem=recv_sem.at[n // GROUP],
            device_id=target(me, n),
            device_id_type=MESH,
        ).start()

    for p in range(CAP):
        incoming[DEVICES - 1, p] = blocks[index_s[p, DEVICES - 1]]

    @pl.loop(0, GROUPS)
    def _(g):
        @pl.when(g < GROUPS - 1)
        def _():
            arrived = incoming.at[pl.ds(g * GROUP, GROUP)]
            pltpu.make_async_copy(arrived, arrived, recv_sem.at[g]).wait()

        @pl.when(g == GROUPS - 1)
        def _():
            arrived = incoming.at[pl.ds(DEVICES - GROUP, GROUP - 1)]
            pltpu.make_async_copy(arrived, arrived, recv_sem.at[g]).wait()

        for p in range(CAP):
            parts = incoming[pl.ds(g * GROUP, GROUP), p].reshape(GROUP * Q, W)
            swapped = jnp.dot(swap, parts, preferred_element_type=jnp.float32).astype(jnp.bfloat16)
            where = pl.ds(pl.multiple_of(p * DEVICES + g * GROUP, GROUP), GROUP)
            for q in range(Q):
                members[where, q * W : (q + 1) * W] = swapped[q * GROUP : (q + 1) * GROUP]

    gram[...] = jnp.zeros_like(gram)

    @pl.loop(0, 8)
    def _(k):
        part = members[:, pl.ds(pl.multiple_of(k * 512, 512), 512)]
        gram[...] += lax.dot_general(part, part, (((1,), (1,)), ((), ())), preferred_element_type=jnp.float32)

    places = CAP * DEVICES
    i = lax.broadcasted_iota(jnp.int32, (places, places), 0)
    j = lax.broadcasted_iota(jnp.int32, (places, places), 1)
    products = gram[...]
    own = jnp.where(i == j, products, 0.0)
    squares_i, squares_j = jnp.sum(own, axis=1, keepdims=True), jnp.sum(own, axis=0, keepdims=True)
    scores = products * lax.rsqrt(squares_i + 1e-06) * lax.rsqrt(squares_j + 1e-06)
    allowed = (squares_j < EMPTY_SQUARES) & (i != j)
    best = jnp.max(jnp.where(allowed, scores, -1.0), axis=1, keepdims=True)
    by_place = jnp.where(
        lanes == 0, best[:DEVICES], jnp.where(lanes == 1, best[DEVICES : 2 * DEVICES], best[2 * DEVICES :])
    )
    highest[...] = by_place.reshape(DEVICES, 1, 128)
    returned[DEVICES - 1] = by_place[DEVICES - 1 :]

    @pl.loop(0, DEVICES - 1)
    def _(n):
        pltpu.make_async_remote_copy(
            src_ref=highest.at[n],
            dst_ref=returned.at[n],
            send_sem=back_send_sem,
            recv_sem=back_recv_sem,
            device_id=origin(me, n),
            device_id_type=MESH,
        ).start()

    sent = outgoing.at[pl.ds(0, DEVICES - 1)]
    pltpu.make_async_copy(sent, sent, send_sem).wait()
    back = returned.at[pl.ds(0, DEVICES - 1)]
    pltpu.make_async_copy(back, back, back_recv_sem).wait()
    pltpu.make_async_copy(back, back, back_send_sem).wait()

    mine = jnp.dot(
        named.astype(jnp.float32),
        returned[...].reshape(DEVICES, 128),
        precision=lax.Precision.HIGHEST,
        preferred_element_type=jnp.float32,
    )
    column = jnp.sum(jnp.where(lanes == place.astype(jnp.int32), mine, 0.0), axis=1, keepdims=True)
    out_ref[...] = jnp.sum(jnp.where(rows == lanes, column, 0.0), axis=0, keepdims=True)


def body(embeddings, cluster_ids):
    vmem = pl.BlockSpec(memory_space=pltpu.VMEM)
    out = pl.pallas_call(
        kernel,
        out_shape=jax.ShapeDtypeStruct((1, ROWS), jnp.float32),
        in_specs=[vmem, vmem],
        out_specs=vmem,
        scratch_shapes=[
            pltpu.VMEM((ROWS + 1, Q, W), jnp.bfloat16),
            pltpu.VMEM((DEVICES, CAP, Q, W), jnp.bfloat16),
            pltpu.VMEM((DEVICES, CAP, Q, W), jnp.bfloat16),
            pltpu.VMEM((CAP * DEVICES, D), jnp.bfloat16),
            pltpu.VMEM((CAP * DEVICES, CAP * DEVICES), jnp.float32),
            pltpu.VMEM((8, 128), jnp.int32),
            pltpu.SMEM((8, 128), jnp.int32),
            pltpu.VMEM((DEVICES, 1, 128), jnp.float32),
            pltpu.VMEM((DEVICES, 1, 128), jnp.float32),
            pltpu.SemaphoreType.DMA,
            pltpu.SemaphoreType.DMA,
            pltpu.SemaphoreType.DMA((GROUPS,)),
            pltpu.SemaphoreType.DMA,
            pltpu.SemaphoreType.DMA,
        ],
        compiler_params=pltpu.CompilerParams(
            collective_id=0, has_side_effects=True, vmem_limit_bytes=40 * 1024 * 1024
        ),
    )(cluster_ids, embeddings)
    return out.reshape(ROWS)


def solution(mesh):
    return jax.shard_map(
        body,
        mesh=mesh,
        in_specs=(P(("doc", "clu"), None), P(("doc", "clu"), None)),
        out_specs=P(("doc", "clu")),
        check_vma=False,
    )
```

```python
import random

import jax
import jax.numpy as jnp
from jax import lax
from jax.experimental import pallas as pl
from jax.experimental.pallas import tpu as pltpu
from jax.sharding import PartitionSpec as P

MESH = pl.DeviceIdType.MESH
DEVICES = 128
ROWS = 128
CAP = 3
D = 4096
Q = 16
W = D // Q
GROUP = 16
GROUPS = DEVICES // GROUP
EMPTY = 1.0
EMPTY_SCORE = 2.0


def order():
    every = [(x, z, y, c) for x in range(4) for z in range(4) for y in range(4) for c in range(2)]
    random.Random(0).shuffle(every)
    return sorted(every, key=lambda o: (-sum(min(k, 4 - k) for k in o[:3]), -o[3]))


ORDER = order()


def code(o):
    return ((o[0] * 4 + o[1]) * 4 + o[2]) * 2 + o[3]


def position():
    doc, clu = lax.axis_index("doc"), lax.axis_index("clu")
    return doc, clu // 8, (clu // 2) % 4, clu % 2


class Around:
    def __init__(self, me):
        x, z, y, c = me
        self.x = [(x + k) % 4 for k in range(4)]
        self.z = [((z + k) % 4) * 8 for k in range(4)]
        self.y = [((y + k) % 4) * 2 for k in range(4)]
        self.c = [c, 1 - c]

    def to(self, o):
        return self.x[o[0]], self.z[o[1]] + self.y[o[2]] + self.c[o[3]]

    def back(self, o):
        return self.to((-o[0] % 4, -o[1] % 4, -o[2] % 4, o[3]))


def code_of(cluster, me):
    x, z, y, c = me
    dx = ((cluster >> 5) + (4 - x)) & 3
    dz = ((cluster >> 3) + (4 - z)) & 3
    dy = ((cluster >> 1) + (4 - y)) & 3
    dc = (cluster + c) & 1
    return ((dx * 4 + dz) * 4 + dy) * 2 + dc


def kernel(
    ids_hbm, emb_hbm, out_ref,
    ids_ref, emb_ref, blocks, outgoing, incoming, members, index_v, index_s, highest, returned,
    ids_sem, emb_sem, index_sem, send_sem, recv_sem, back_send_sem, back_recv_sem,
):
    me = position()
    around = Around(me)
    barrier = pltpu.get_barrier_semaphore()

    ids_in = pltpu.make_async_copy(ids_hbm, ids_ref, ids_sem)
    ids_in.start()
    rows_in = []
    for g in range(ROWS // GROUP):
        group = pl.ds(g * GROUP, GROUP)
        rows_in.append(pltpu.make_async_copy(emb_hbm.at[group], emb_ref.at[group], emb_sem.at[g]))
        rows_in[g].start()

    for o in ORDER[:-1]:
        pl.semaphore_signal(barrier, inc=1, device_id=around.back(o), device_id_type=MESH)

    rows = lax.broadcasted_iota(jnp.int32, (ROWS, DEVICES), 0)
    lanes = lax.broadcasted_iota(jnp.int32, (ROWS, DEVICES), 1)
    ids_in.wait()
    codes = code_of(ids_ref[...], me)
    named = jnp.transpose(jnp.broadcast_to(codes, (DEVICES, ROWS))) == lanes
    earlier = jnp.dot(
        (lanes < rows).astype(jnp.bfloat16), named.astype(jnp.bfloat16), preferred_element_type=jnp.float32
    )
    place = jnp.sum(jnp.where(named, earlier, 0.0), axis=1, keepdims=True)
    for p in range(CAP):
        here = named & (earlier == p)
        row = ROWS + jnp.sum(jnp.where(here, rows - ROWS, 0), axis=0, keepdims=True)
        index_v[p : p + 1, :] = jnp.clip(row, 0, ROWS)
    to_scalars = pltpu.make_async_copy(index_v, index_s, index_sem)
    to_scalars.start()

    a = lax.broadcasted_iota(jnp.int32, (GROUP * Q, GROUP * Q), 0)
    b = lax.broadcasted_iota(jnp.int32, (GROUP * Q, GROUP * Q), 1)
    swap = ((a // Q == b % GROUP) & (a % Q == b // GROUP)).astype(jnp.bfloat16)

    blocks[ROWS] = jnp.full((Q, W), EMPTY, jnp.bfloat16)
    for g in range(ROWS // GROUP):
        rows_in[g].wait()
        values = emb_ref[pl.ds(g * GROUP, GROUP)].astype(jnp.float32)
        squares = jnp.sum(values * values, axis=1, keepdims=True)
        normed = (values * lax.rsqrt(squares + 1e-06)).astype(jnp.bfloat16)
        parts = jnp.concatenate([normed[:, q * W : (q + 1) * W] for q in range(Q)], axis=0)
        swapped = jnp.dot(swap, parts, preferred_element_type=jnp.float32).astype(jnp.bfloat16)
        blocks[pl.ds(g * GROUP, GROUP)] = swapped.reshape(GROUP, Q, W)

    to_scalars.wait()
    pl.semaphore_wait(barrier, DEVICES - 1)

    for n, o in enumerate(ORDER[:-1]):
        for p in range(CAP):
            outgoing[n, p] = blocks[index_s[p, code(o)]]
        pltpu.make_async_remote_copy(
            src_ref=outgoing.at[n],
            dst_ref=incoming.at[n],
            send_sem=send_sem,
            recv_sem=recv_sem.at[n // GROUP],
            device_id=around.to(o),
            device_id_type=MESH,
        ).start()

    for p in range(CAP):
        incoming[DEVICES - 1, p] = blocks[index_s[p, 0]]

    def arrive(g, count):
        arrived = incoming.at[pl.ds(g * GROUP, count)]
        pltpu.make_async_copy(arrived, arrived, recv_sem.at[g]).wait()
        for p in range(CAP):
            parts = incoming[pl.ds(g * GROUP, GROUP), p].reshape(GROUP * Q, W)
            swapped = jnp.dot(swap, parts, preferred_element_type=jnp.float32).astype(jnp.bfloat16)
            where = pl.ds(pl.multiple_of(p * DEVICES + g * GROUP, GROUP), GROUP)
            for q in range(Q):
                members[where, q * W : (q + 1) * W] = swapped[q * GROUP : (q + 1) * GROUP]

    @pl.loop(0, GROUPS - 1)
    def _(g):
        arrive(g, GROUP)

    arrive(GROUPS - 1, GROUP - 1)

    places = CAP * DEVICES
    scores = lax.dot_general(
        members[...], members[...], (((1,), (1,)), ((), ())), preferred_element_type=jnp.float32
    )
    i = lax.broadcasted_iota(jnp.int32, (places, places), 0)
    j = lax.broadcasted_iota(jnp.int32, (places, places), 1)
    own = jnp.sum(jnp.where(i == j, scores, 0.0), axis=0, keepdims=True)
    allowed = (own < EMPTY_SCORE) & (i != j)
    best = jnp.max(jnp.where(allowed, scores, -1.0), axis=1, keepdims=True)
    by_place = jnp.where(
        lanes == 0, best[:DEVICES], jnp.where(lanes == 1, best[DEVICES : 2 * DEVICES], best[2 * DEVICES :])
    )
    highest[...] = by_place.reshape(DEVICES, 1, 128)
    returned[0] = by_place[DEVICES - 1 :]

    for n, o in enumerate(ORDER[:-1]):
        pltpu.make_async_remote_copy(
            src_ref=highest.at[n],
            dst_ref=returned.at[code(o)],
            send_sem=back_send_sem,
            recv_sem=back_recv_sem,
            device_id=around.back(o),
            device_id_type=MESH,
        ).start()

    back = returned.at[pl.ds(1, DEVICES - 1)]
    pltpu.make_async_copy(back, back, back_recv_sem).wait()

    mine = jnp.dot(
        named.astype(jnp.float32),
        returned[...].reshape(DEVICES, 128),
        precision=lax.Precision.HIGHEST,
        preferred_element_type=jnp.float32,
    )
    column = jnp.sum(jnp.where(lanes == place.astype(jnp.int32), mine, 0.0), axis=1, keepdims=True)
    out_ref[...] = jnp.sum(jnp.where(rows == lanes, column, 0.0), axis=0, keepdims=True)

    sent = outgoing.at[pl.ds(0, DEVICES - 1)]
    pltpu.make_async_copy(sent, sent, send_sem).wait()
    pltpu.make_async_copy(back, back, back_send_sem).wait()


def body(embeddings, cluster_ids):
    hbm = pl.BlockSpec(memory_space=pltpu.HBM)
    out = pl.pallas_call(
        kernel,
        out_shape=jax.ShapeDtypeStruct((1, ROWS), jnp.float32),
        in_specs=[hbm, hbm],
        out_specs=pl.BlockSpec(memory_space=pltpu.VMEM),
        scratch_shapes=[
            pltpu.VMEM((1, ROWS), jnp.int32),
            pltpu.VMEM((ROWS, D), jnp.bfloat16),
            pltpu.VMEM((ROWS + 1, Q, W), jnp.bfloat16),
            pltpu.VMEM((DEVICES, CAP, Q, W), jnp.bfloat16),
            pltpu.VMEM((DEVICES, CAP, Q, W), jnp.bfloat16),
            pltpu.VMEM((CAP * DEVICES, D), jnp.bfloat16),
            pltpu.VMEM((8, 128), jnp.int32),
            pltpu.SMEM((8, 128), jnp.int32),
            pltpu.VMEM((DEVICES, 1, 128), jnp.float32),
            pltpu.VMEM((DEVICES, 1, 128), jnp.float32),
            pltpu.SemaphoreType.DMA,
            pltpu.SemaphoreType.DMA((ROWS // GROUP,)),
            pltpu.SemaphoreType.DMA,
            pltpu.SemaphoreType.DMA,
            pltpu.SemaphoreType.DMA((GROUPS,)),
            pltpu.SemaphoreType.DMA,
            pltpu.SemaphoreType.DMA,
        ],
        compiler_params=pltpu.CompilerParams(
            collective_id=0, has_side_effects=True, vmem_limit_bytes=62 * 1024 * 1024
        ),
    )(cluster_ids.reshape(1, ROWS), embeddings)
    return out.reshape(ROWS)


def solution(mesh):
    return jax.shard_map(
        body,
        mesh=mesh,
        in_specs=(P(("doc", "clu"), None), P(("doc", "clu"), None)),
        out_specs=P(("doc", "clu")),
        check_vma=False,
    )
```

```python
import random

import jax
import jax.numpy as jnp
from jax import lax
from jax.experimental import pallas as pl
from jax.experimental.pallas import tpu as pltpu
from jax.sharding import PartitionSpec as P

MESH = pl.DeviceIdType.MESH
DEVICES = 128
ROWS = 128
CAP = 3
D = 4096
Q = 16
W = D // Q
GROUP = 16
GROUPS = DEVICES // GROUP
EMPTY = 1.0
EMPTY_SCORE = 2.0


WHEN = (3, 2, 0, 1)


def axes(o):
    return sum(k != 0 for k in o[:3])


def order():
    every = [(x, z, y, c) for x in range(4) for z in range(4) for y in range(4) for c in range(2)]
    random.Random(0).shuffle(every)
    distance = lambda o: sum(min(k, 4 - k) for k in o[:3])
    return sorted(every, key=lambda o: (WHEN[axes(o)], -distance(o), -o[3]))


ORDER = order()
FIRST = 54


def code(o):
    return ((o[0] * 4 + o[1]) * 4 + o[2]) * 2 + o[3]


def position():
    doc, clu = lax.axis_index("doc"), lax.axis_index("clu")
    return doc, clu // 8, (clu // 2) % 4, clu % 2


class Around:
    def __init__(self, me):
        x, z, y, c = me
        self.x = [(x + k) % 4 for k in range(4)]
        self.z = [((z + k) % 4) * 8 for k in range(4)]
        self.y = [((y + k) % 4) * 2 for k in range(4)]
        self.c = [c, 1 - c]

    def to(self, o):
        return self.x[o[0]], self.z[o[1]] + self.y[o[2]] + self.c[o[3]]

    def back(self, o):
        return self.to((-o[0] % 4, -o[1] % 4, -o[2] % 4, o[3]))


def code_of(cluster, me):
    x, z, y, c = me
    dx = ((cluster >> 5) + (4 - x)) & 3
    dz = ((cluster >> 3) + (4 - z)) & 3
    dy = ((cluster >> 1) + (4 - y)) & 3
    dc = (cluster + c) & 1
    return ((dx * 4 + dz) * 4 + dy) * 2 + dc


def kernel(
    ids_hbm, emb_hbm, out_ref,
    ids_ref, emb_ref, blocks, outgoing, incoming, members, index_v, index_s, highest, returned,
    ids_sem, emb_sem, index_sem, send_sem, recv_sem, back_send_sem, back_recv_sem, entered,
):
    me = position()
    around = Around(me)
    barrier = pltpu.get_barrier_semaphore()

    ids_in = pltpu.make_async_copy(ids_hbm, ids_ref, ids_sem)
    ids_in.start()
    rows_in = pltpu.make_async_copy(emb_hbm, emb_ref, emb_sem)
    rows_in.start()

    planes = [o for o in ORDER[:-1] if axes(o) < 3]
    for o in planes:
        pl.semaphore_signal(barrier, inc=1, device_id=around.back(o), device_id_type=MESH)

    rows = lax.broadcasted_iota(jnp.int32, (ROWS, DEVICES), 0)
    lanes = lax.broadcasted_iota(jnp.int32, (ROWS, DEVICES), 1)
    ids_in.wait()
    codes = code_of(ids_ref[...], me)
    named = jnp.transpose(jnp.broadcast_to(codes, (DEVICES, ROWS))) == lanes
    earlier = jnp.dot(
        (lanes < rows).astype(jnp.bfloat16), named.astype(jnp.bfloat16), preferred_element_type=jnp.float32
    )
    place = jnp.sum(jnp.where(named, earlier, 0.0), axis=1, keepdims=True)
    for p in range(CAP):
        here = named & (earlier == p)
        row = ROWS + jnp.sum(jnp.where(here, rows - ROWS, 0), axis=0, keepdims=True)
        index_v[p : p + 1, :] = jnp.clip(row, 0, ROWS)
    to_scalars = pltpu.make_async_copy(index_v, index_s, index_sem)
    to_scalars.start()

    a = lax.broadcasted_iota(jnp.int32, (GROUP * Q, GROUP * Q), 0)
    b = lax.broadcasted_iota(jnp.int32, (GROUP * Q, GROUP * Q), 1)
    swap = ((a // Q == b % GROUP) & (a % Q == b // GROUP)).astype(jnp.bfloat16)

    blocks[ROWS] = jnp.full((Q, W), EMPTY, jnp.bfloat16)
    rows_in.wait()
    for g in range(ROWS // GROUP):
        values = emb_ref[pl.ds(g * GROUP, GROUP)].astype(jnp.float32)
        squares = jnp.sum(values * values, axis=1, keepdims=True)
        normed = (values * lax.rsqrt(squares + 1e-06)).astype(jnp.bfloat16)
        parts = jnp.concatenate([normed[:, q * W : (q + 1) * W] for q in range(Q)], axis=0)
        swapped = jnp.dot(swap, parts, preferred_element_type=jnp.float32).astype(jnp.bfloat16)
        blocks[pl.ds(g * GROUP, GROUP)] = swapped.reshape(GROUP, Q, W)

    to_scalars.wait()
    pl.semaphore_wait(barrier, len(planes))
    for k in range(1, 4):
        pl.semaphore_signal(entered, inc=1, device_id=around.to((k, 0, 0, 0)), device_id_type=MESH)

    for n, o in enumerate(ORDER[:-1]):
        if n == FIRST:
            pl.semaphore_wait(entered, 3)
        for p in range(CAP):
            outgoing[n, p] = blocks[index_s[p, code(o)]]
        pltpu.make_async_remote_copy(
            src_ref=outgoing.at[n],
            dst_ref=incoming.at[n],
            send_sem=send_sem,
            recv_sem=recv_sem.at[n // GROUP],
            device_id=around.to(o),
            device_id_type=MESH,
        ).start()

    for p in range(CAP):
        incoming[DEVICES - 1, p] = blocks[index_s[p, 0]]

    def arrive(g, count):
        arrived = incoming.at[pl.ds(g * GROUP, count)]
        pltpu.make_async_copy(arrived, arrived, recv_sem.at[g]).wait()
        for p in range(CAP):
            parts = incoming[pl.ds(g * GROUP, GROUP), p].reshape(GROUP * Q, W)
            swapped = jnp.dot(swap, parts, preferred_element_type=jnp.float32).astype(jnp.bfloat16)
            where = pl.ds(pl.multiple_of(p * DEVICES + g * GROUP, GROUP), GROUP)
            for q in range(Q):
                members[where, q * W : (q + 1) * W] = swapped[q * GROUP : (q + 1) * GROUP]

    @pl.loop(0, GROUPS - 1)
    def _(g):
        arrive(g, GROUP)

    arrive(GROUPS - 1, GROUP - 1)

    places = CAP * DEVICES
    scores = lax.dot_general(
        members[...], members[...], (((1,), (1,)), ((), ())), preferred_element_type=jnp.float32
    )
    i = lax.broadcasted_iota(jnp.int32, (places, places), 0)
    j = lax.broadcasted_iota(jnp.int32, (places, places), 1)
    own = jnp.sum(jnp.where(i == j, scores, 0.0), axis=0, keepdims=True)
    allowed = (own < EMPTY_SCORE) & (i != j)
    best = jnp.max(jnp.where(allowed, scores, -1.0), axis=1, keepdims=True)
    by_place = jnp.where(
        lanes == 0, best[:DEVICES], jnp.where(lanes == 1, best[DEVICES : 2 * DEVICES], best[2 * DEVICES :])
    )
    highest[...] = by_place.reshape(DEVICES, 1, 128)
    returned[0] = by_place[DEVICES - 1 :]

    for n, o in enumerate(ORDER[:-1]):
        pltpu.make_async_remote_copy(
            src_ref=highest.at[n],
            dst_ref=returned.at[code(o)],
            send_sem=back_send_sem,
            recv_sem=back_recv_sem,
            device_id=around.back(o),
            device_id_type=MESH,
        ).start()

    back = returned.at[pl.ds(1, DEVICES - 1)]
    pltpu.make_async_copy(back, back, back_recv_sem).wait()

    mine = jnp.dot(
        named.astype(jnp.float32),
        returned[...].reshape(DEVICES, 128),
        precision=lax.Precision.HIGHEST,
        preferred_element_type=jnp.float32,
    )
    column = jnp.sum(jnp.where(lanes == place.astype(jnp.int32), mine, 0.0), axis=1, keepdims=True)
    out_ref[...] = jnp.sum(jnp.where(rows == lanes, column, 0.0), axis=0, keepdims=True)

    sent = outgoing.at[pl.ds(0, DEVICES - 1)]
    pltpu.make_async_copy(sent, sent, send_sem).wait()
    pltpu.make_async_copy(back, back, back_send_sem).wait()


def body(embeddings, cluster_ids):
    hbm = pl.BlockSpec(memory_space=pltpu.HBM)
    out = pl.pallas_call(
        kernel,
        out_shape=jax.ShapeDtypeStruct((1, ROWS), jnp.float32),
        in_specs=[hbm, hbm],
        out_specs=pl.BlockSpec(memory_space=pltpu.VMEM),
        scratch_shapes=[
            pltpu.VMEM((1, ROWS), jnp.int32),
            pltpu.VMEM((ROWS, D), jnp.bfloat16),
            pltpu.VMEM((ROWS + 1, Q, W), jnp.bfloat16),
            pltpu.VMEM((DEVICES, CAP, Q, W), jnp.bfloat16),
            pltpu.VMEM((DEVICES, CAP, Q, W), jnp.bfloat16),
            pltpu.VMEM((CAP * DEVICES, D), jnp.bfloat16),
            pltpu.VMEM((8, 128), jnp.int32),
            pltpu.SMEM((8, 128), jnp.int32),
            pltpu.VMEM((DEVICES, 1, 128), jnp.float32),
            pltpu.VMEM((DEVICES, 1, 128), jnp.float32),
            pltpu.SemaphoreType.DMA,
            pltpu.SemaphoreType.DMA,
            pltpu.SemaphoreType.DMA,
            pltpu.SemaphoreType.DMA,
            pltpu.SemaphoreType.DMA((GROUPS,)),
            pltpu.SemaphoreType.DMA,
            pltpu.SemaphoreType.DMA,
            pltpu.SemaphoreType.REGULAR,
        ],
        compiler_params=pltpu.CompilerParams(
            collective_id=0, has_side_effects=True, vmem_limit_bytes=40 * 1024 * 1024
        ),
    )(
        pltpu.with_memory_space_constraint(cluster_ids.reshape(1, ROWS), pltpu.HBM),
        pltpu.with_memory_space_constraint(embeddings, pltpu.HBM),
    )
    return out.reshape(ROWS)


def solution(mesh):
    return jax.shard_map(
        body,
        mesh=mesh,
        in_specs=(P(("doc", "clu"), None), P(("doc", "clu"), None)),
        out_specs=P(("doc", "clu")),
        check_vma=False,
    )
```

```python
import random

import jax
import jax.numpy as jnp
from jax import lax
from jax.experimental import pallas as pl
from jax.experimental.pallas import tpu as pltpu
from jax.sharding import PartitionSpec as P

MESH = pl.DeviceIdType.MESH
DEVICES = 128
ROWS = 128
CAP = 3
D = 4096
Q = 16
W = D // Q
GROUP = 16
GROUPS = DEVICES // GROUP
EMPTY = 1.0
EMPTY_SCORE = 2.0


WHEN = (3, 2, 0, 1)


def axes(o):
    return sum(k != 0 for k in o[:3])


def distance(o):
    return sum(min(k, 4 - k) for k in o[:3])


def order():
    every = [(x, z, y, c) for x in range(4) for z in range(4) for y in range(4) for c in range(2)]
    random.Random(0).shuffle(every)
    return sorted(every, key=lambda o: (WHEN[axes(o)], -distance(o), -o[3]))


ORDER = order()
FIRST = 54


def code(o):
    return ((o[0] * 4 + o[1]) * 4 + o[2]) * 2 + o[3]


def position():
    doc, clu = lax.axis_index("doc"), lax.axis_index("clu")
    return doc, clu // 8, (clu // 2) % 4, clu % 2


class Around:
    def __init__(self, me):
        x, z, y, c = me
        self.x = [(x + k) % 4 for k in range(4)]
        self.z = [((z + k) % 4) * 8 for k in range(4)]
        self.y = [((y + k) % 4) * 2 for k in range(4)]
        self.c = [c, 1 - c]

    def to(self, o):
        return self.x[o[0]], self.z[o[1]] + self.y[o[2]] + self.c[o[3]]

    def back(self, o):
        return self.to((-o[0] % 4, -o[1] % 4, -o[2] % 4, o[3]))


def code_of(cluster, me):
    x, z, y, c = me
    dx = ((cluster >> 5) + (4 - x)) & 3
    dz = ((cluster >> 3) + (4 - z)) & 3
    dy = ((cluster >> 1) + (4 - y)) & 3
    dc = (cluster + c) & 1
    return ((dx * 4 + dz) * 4 + dy) * 2 + dc


def kernel(
    ids_hbm, emb_hbm, out_ref,
    ids_ref, emb_ref, blocks, outgoing, incoming, members, index_v, index_s, highest, returned,
    ids_sem, emb_sem, index_sem, send_sem, recv_sem, back_send_sem, back_recv_sem, entered,
):
    me = position()
    around = Around(me)
    barrier = pltpu.get_barrier_semaphore()

    ids_in = pltpu.make_async_copy(ids_hbm, ids_ref, ids_sem)
    ids_in.start()
    rows_in = pltpu.make_async_copy(emb_hbm, emb_ref, emb_sem)
    rows_in.start()

    planes = [o for o in ORDER[:-1] if axes(o) < 3]
    for o in planes:
        pl.semaphore_signal(barrier, inc=1, device_id=around.back(o), device_id_type=MESH)

    rows = lax.broadcasted_iota(jnp.int32, (ROWS, DEVICES), 0)
    lanes = lax.broadcasted_iota(jnp.int32, (ROWS, DEVICES), 1)
    ids_in.wait()
    codes = code_of(ids_ref[...], me)
    named = jnp.transpose(jnp.broadcast_to(codes, (DEVICES, ROWS))) == lanes
    earlier = jnp.dot(
        (lanes < rows).astype(jnp.bfloat16), named.astype(jnp.bfloat16), preferred_element_type=jnp.float32
    )
    place = jnp.sum(jnp.where(named, earlier, 0.0), axis=1, keepdims=True)
    for p in range(CAP):
        here = named & (earlier == p)
        row = ROWS + jnp.sum(jnp.where(here, rows - ROWS, 0), axis=0, keepdims=True)
        index_v[p : p + 1, :] = jnp.clip(row, 0, ROWS)
    to_scalars = pltpu.make_async_copy(index_v, index_s, index_sem)
    to_scalars.start()

    a = lax.broadcasted_iota(jnp.int32, (GROUP * Q, GROUP * Q), 0)
    b = lax.broadcasted_iota(jnp.int32, (GROUP * Q, GROUP * Q), 1)
    swap = ((a // Q == b % GROUP) & (a % Q == b // GROUP)).astype(jnp.bfloat16)

    blocks[ROWS] = jnp.full((Q, W), EMPTY, jnp.bfloat16)
    rows_in.wait()
    for g in range(ROWS // GROUP):
        values = emb_ref[pl.ds(g * GROUP, GROUP)].astype(jnp.float32)
        squares = jnp.sum(values * values, axis=1, keepdims=True)
        normed = (values * lax.rsqrt(squares + 1e-06)).astype(jnp.bfloat16)
        parts = jnp.concatenate([normed[:, q * W : (q + 1) * W] for q in range(Q)], axis=0)
        swapped = jnp.dot(swap, parts, preferred_element_type=jnp.float32).astype(jnp.bfloat16)
        blocks[pl.ds(g * GROUP, GROUP)] = swapped.reshape(GROUP, Q, W)

    to_scalars.wait()
    pl.semaphore_wait(barrier, len(planes))
    for k in range(1, 4):
        pl.semaphore_signal(entered, inc=1, device_id=around.to((k, 0, 0, 0)), device_id_type=MESH)

    for n, o in enumerate(ORDER[:-1]):
        if n == FIRST:
            pl.semaphore_wait(entered, 3)
        for p in range(CAP):
            outgoing[n, p] = blocks[index_s[p, code(o)]]
        pltpu.make_async_remote_copy(
            src_ref=outgoing.at[n],
            dst_ref=incoming.at[n],
            send_sem=send_sem,
            recv_sem=recv_sem.at[n // GROUP],
            device_id=around.to(o),
            device_id_type=MESH,
        ).start()

    for p in range(CAP):
        incoming[DEVICES - 1, p] = blocks[index_s[p, 0]]

    def arrive(g, count):
        arrived = incoming.at[pl.ds(g * GROUP, count)]
        pltpu.make_async_copy(arrived, arrived, recv_sem.at[g]).wait()
        for p in range(CAP):
            parts = incoming[pl.ds(g * GROUP, GROUP), p].reshape(GROUP * Q, W)
            swapped = jnp.dot(swap, parts, preferred_element_type=jnp.float32).astype(jnp.bfloat16)
            where = pl.ds(pl.multiple_of(p * DEVICES + g * GROUP, GROUP), GROUP)
            for q in range(Q):
                members[where, q * W : (q + 1) * W] = swapped[q * GROUP : (q + 1) * GROUP]

    @pl.loop(0, GROUPS - 1)
    def _(g):
        arrive(g, GROUP)

    arrive(GROUPS - 1, GROUP - 1)

    split = 2 * DEVICES
    places = CAP * DEVICES
    scores = lax.dot_general(
        members[...], members[:split], (((1,), (1,)), ((), ())), preferred_element_type=jnp.float32
    )
    corner = lax.dot_general(
        members[split:], members[split:], (((1,), (1,)), ((), ())), preferred_element_type=jnp.float32
    )
    i = lax.broadcasted_iota(jnp.int32, (places, split), 0)
    j = lax.broadcasted_iota(jnp.int32, (places, split), 1)
    first = jnp.sum(jnp.where(i == j, scores, 0.0), axis=0, keepdims=True) < EMPTY_SCORE
    own = jnp.where(rows == lanes, corner, 0.0)
    last = jnp.sum(own, axis=0, keepdims=True) < EMPTY_SCORE
    last_rows = jnp.sum(own, axis=1, keepdims=True) < EMPTY_SCORE
    best = jnp.max(jnp.where(first & (i != j), scores, -1.0), axis=1, keepdims=True)
    across = jnp.max(jnp.where(last_rows, scores[split:], -1.0), axis=0, keepdims=True)
    turned = [
        jnp.max(jnp.where(rows == lanes, across[:, k * DEVICES : (k + 1) * DEVICES], -1.0), axis=1, keepdims=True)
        for k in range(2)
    ]
    inside = jnp.max(jnp.where(last & (rows != lanes), corner, -1.0), axis=1, keepdims=True)
    best = jnp.maximum(best, jnp.concatenate([*turned, inside], axis=0))
    by_place = jnp.where(
        lanes == 0, best[:DEVICES], jnp.where(lanes == 1, best[DEVICES : 2 * DEVICES], best[2 * DEVICES :])
    )
    highest[...] = by_place.reshape(DEVICES, 1, 128)
    returned[0] = by_place[DEVICES - 1 :]

    for o in sorted(ORDER[:-1], key=distance, reverse=True):
        pltpu.make_async_remote_copy(
            src_ref=highest.at[ORDER.index(o)],
            dst_ref=returned.at[code(o)],
            send_sem=back_send_sem,
            recv_sem=back_recv_sem,
            device_id=around.back(o),
            device_id_type=MESH,
        ).start()

    back = returned.at[pl.ds(1, DEVICES - 1)]
    pltpu.make_async_copy(back, back, back_recv_sem).wait()

    mine = jnp.dot(
        named.astype(jnp.float32),
        returned[...].reshape(DEVICES, 128),
        precision=lax.Precision.HIGHEST,
        preferred_element_type=jnp.float32,
    )
    column = jnp.sum(jnp.where(lanes == place.astype(jnp.int32), mine, 0.0), axis=1, keepdims=True)
    out_ref[...] = jnp.sum(jnp.where(rows == lanes, column, 0.0), axis=0, keepdims=True)

    sent = outgoing.at[pl.ds(0, DEVICES - 1)]
    pltpu.make_async_copy(sent, sent, send_sem).wait()
    pltpu.make_async_copy(back, back, back_send_sem).wait()


def body(embeddings, cluster_ids):
    hbm = pl.BlockSpec(memory_space=pltpu.HBM)
    out = pl.pallas_call(
        kernel,
        out_shape=jax.ShapeDtypeStruct((1, ROWS), jnp.float32),
        in_specs=[hbm, hbm],
        out_specs=pl.BlockSpec(memory_space=pltpu.VMEM),
        scratch_shapes=[
            pltpu.VMEM((1, ROWS), jnp.int32),
            pltpu.VMEM((ROWS, D), jnp.bfloat16),
            pltpu.VMEM((ROWS + 1, Q, W), jnp.bfloat16),
            pltpu.VMEM((DEVICES, CAP, Q, W), jnp.bfloat16),
            pltpu.VMEM((DEVICES, CAP, Q, W), jnp.bfloat16),
            pltpu.VMEM((CAP * DEVICES, D), jnp.bfloat16),
            pltpu.VMEM((8, 128), jnp.int32),
            pltpu.SMEM((8, 128), jnp.int32),
            pltpu.VMEM((DEVICES, 1, 128), jnp.float32),
            pltpu.VMEM((DEVICES, 1, 128), jnp.float32),
            pltpu.SemaphoreType.DMA,
            pltpu.SemaphoreType.DMA,
            pltpu.SemaphoreType.DMA,
            pltpu.SemaphoreType.DMA,
            pltpu.SemaphoreType.DMA((GROUPS,)),
            pltpu.SemaphoreType.DMA,
            pltpu.SemaphoreType.DMA,
            pltpu.SemaphoreType.REGULAR,
        ],
        compiler_params=pltpu.CompilerParams(
            collective_id=0, has_side_effects=True, vmem_limit_bytes=40 * 1024 * 1024
        ),
    )(
        pltpu.with_memory_space_constraint(cluster_ids.reshape(1, ROWS), pltpu.HBM),
        pltpu.with_memory_space_constraint(embeddings, pltpu.HBM),
    )
    return out.reshape(ROWS)


def solution(mesh):
    return jax.shard_map(
        body,
        mesh=mesh,
        in_specs=(P(("doc", "clu"), None), P(("doc", "clu"), None)),
        out_specs=P(("doc", "clu")),
        check_vma=False,
    )
```

```python
import random

import jax
import jax.numpy as jnp
from jax import lax
from jax.experimental import pallas as pl
from jax.experimental.pallas import tpu as pltpu
from jax.sharding import PartitionSpec as P

MESH = pl.DeviceIdType.MESH
DEVICES = 128
ROWS = 128
CAP = 3
D = 4096
Q = 16
W = D // Q
GROUP = 16
GROUPS = DEVICES // GROUP
EMPTY = 1.0
EMPTY_SCORE = 2.0


def axes(o):
    return sum(k != 0 for k in o[:3])


def distance(o):
    return sum(min(k, 4 - k) for k in o[:3])


def turn(o):
    return (4, 0, 1 if distance(o) > 2 else 3, 2)[axes(o)]


def order():
    every = [(x, z, y, c) for x in range(4) for z in range(4) for y in range(4) for c in range(2)]
    random.Random(0).shuffle(every)
    return sorted(every, key=lambda o: (turn(o), -o[3], -distance(o)))


ORDER = order()
TWO = [turn(o) for o in ORDER].index(1)
THREE = [turn(o) for o in ORDER].index(2)


def code(o):
    return ((o[0] * 4 + o[1]) * 4 + o[2]) * 2 + o[3]


def position():
    doc, clu = lax.axis_index("doc"), lax.axis_index("clu")
    return doc, clu // 8, (clu // 2) % 4, clu % 2


class Around:
    def __init__(self, me):
        x, z, y, c = me
        self.x = [(x + k) % 4 for k in range(4)]
        self.z = [((z + k) % 4) * 8 for k in range(4)]
        self.y = [((y + k) % 4) * 2 for k in range(4)]
        self.c = [c, 1 - c]

    def to(self, o):
        return self.x[o[0]], self.z[o[1]] + self.y[o[2]] + self.c[o[3]]

    def back(self, o):
        return self.to((-o[0] % 4, -o[1] % 4, -o[2] % 4, o[3]))


def code_of(cluster, me):
    x, z, y, c = me
    dx = ((cluster >> 5) + (4 - x)) & 3
    dz = ((cluster >> 3) + (4 - z)) & 3
    dy = ((cluster >> 1) + (4 - y)) & 3
    dc = (cluster + c) & 1
    return ((dx * 4 + dz) * 4 + dy) * 2 + dc


def kernel(
    ids_hbm, emb_hbm, out_ref,
    ids_ref, emb_ref, blocks, outgoing, incoming, members, index_v, index_s, highest, returned,
    ids_sem, emb_sem, index_sem, send_sem, recv_sem, back_send_sem, back_recv_sem, lines_known, planes_known,
):
    me = position()
    around = Around(me)
    barrier = pltpu.get_barrier_semaphore()

    ids_in = pltpu.make_async_copy(ids_hbm, ids_ref, ids_sem)
    ids_in.start()
    rows_in = pltpu.make_async_copy(emb_hbm, emb_ref, emb_sem)
    rows_in.start()

    lines = [o for o in ORDER[:-1] if axes(o) < 2]
    for o in lines:
        pl.semaphore_signal(barrier, inc=1, device_id=around.back(o), device_id_type=MESH)

    rows = lax.broadcasted_iota(jnp.int32, (ROWS, DEVICES), 0)
    lanes = lax.broadcasted_iota(jnp.int32, (ROWS, DEVICES), 1)
    ids_in.wait()
    codes = code_of(ids_ref[...], me)
    named = jnp.transpose(jnp.broadcast_to(codes, (DEVICES, ROWS))) == lanes
    earlier = jnp.dot(
        (lanes < rows).astype(jnp.bfloat16), named.astype(jnp.bfloat16), preferred_element_type=jnp.float32
    )
    place = jnp.sum(jnp.where(named, earlier, 0.0), axis=1, keepdims=True)
    for p in range(CAP):
        here = named & (earlier == p)
        row = ROWS + jnp.sum(jnp.where(here, rows - ROWS, 0), axis=0, keepdims=True)
        index_v[p : p + 1, :] = jnp.clip(row, 0, ROWS)
    to_scalars = pltpu.make_async_copy(index_v, index_s, index_sem)
    to_scalars.start()

    a = lax.broadcasted_iota(jnp.int32, (GROUP * Q, GROUP * Q), 0)
    b = lax.broadcasted_iota(jnp.int32, (GROUP * Q, GROUP * Q), 1)
    swap = ((a // Q == b % GROUP) & (a % Q == b // GROUP)).astype(jnp.bfloat16)

    blocks[ROWS] = jnp.full((Q, W), EMPTY, jnp.bfloat16)
    rows_in.wait()
    for g in range(ROWS // GROUP):
        values = emb_ref[pl.ds(g * GROUP, GROUP)].astype(jnp.float32)
        squares = jnp.sum(values * values, axis=1, keepdims=True)
        normed = (values * lax.rsqrt(squares + 1e-06)).astype(jnp.bfloat16)
        parts = jnp.concatenate([normed[:, q * W : (q + 1) * W] for q in range(Q)], axis=0)
        swapped = jnp.dot(swap, parts, preferred_element_type=jnp.float32).astype(jnp.bfloat16)
        blocks[pl.ds(g * GROUP, GROUP)] = swapped.reshape(GROUP, Q, W)

    to_scalars.wait()
    pl.semaphore_wait(barrier, len(lines))
    for k in range(1, 4):
        for peer in ((k, 0, 0, 0), (0, 0, k, 0)):
            pl.semaphore_signal(lines_known, inc=1, device_id=around.to(peer), device_id_type=MESH)
    for n, o in enumerate(ORDER[:-1]):
        if n == TWO:
            pl.semaphore_wait(lines_known, 6)
            for k in range(1, 4):
                pl.semaphore_signal(planes_known, inc=1, device_id=around.to((k, 0, 0, 0)), device_id_type=MESH)
        if n == THREE:
            pl.semaphore_wait(planes_known, 3)
        for p in range(CAP):
            outgoing[n, p] = blocks[index_s[p, code(o)]]
        pltpu.make_async_remote_copy(
            src_ref=outgoing.at[n],
            dst_ref=incoming.at[n],
            send_sem=send_sem,
            recv_sem=recv_sem.at[n // GROUP],
            device_id=around.to(o),
            device_id_type=MESH,
        ).start()

    for p in range(CAP):
        incoming[DEVICES - 1, p] = blocks[index_s[p, 0]]

    def arrive(g, count):
        arrived = incoming.at[pl.ds(g * GROUP, count)]
        pltpu.make_async_copy(arrived, arrived, recv_sem.at[g]).wait()
        for p in range(CAP):
            parts = incoming[pl.ds(g * GROUP, GROUP), p].reshape(GROUP * Q, W)
            swapped = jnp.dot(swap, parts, preferred_element_type=jnp.float32).astype(jnp.bfloat16)
            where = pl.ds(pl.multiple_of(p * DEVICES + g * GROUP, GROUP), GROUP)
            for q in range(Q):
                members[where, q * W : (q + 1) * W] = swapped[q * GROUP : (q + 1) * GROUP]

    @pl.loop(0, GROUPS - 1)
    def _(g):
        arrive(g, GROUP)

    arrive(GROUPS - 1, GROUP - 1)

    split = 2 * DEVICES
    places = CAP * DEVICES
    scores = lax.dot_general(
        members[...], members[:split], (((1,), (1,)), ((), ())), preferred_element_type=jnp.float32
    )
    corner = lax.dot_general(
        members[split:], members[split:], (((1,), (1,)), ((), ())), preferred_element_type=jnp.float32
    )
    i = lax.broadcasted_iota(jnp.int32, (places, split), 0)
    j = lax.broadcasted_iota(jnp.int32, (places, split), 1)
    first = jnp.sum(jnp.where(i == j, scores, 0.0), axis=0, keepdims=True) < EMPTY_SCORE
    own = jnp.where(rows == lanes, corner, 0.0)
    last = jnp.sum(own, axis=0, keepdims=True) < EMPTY_SCORE
    last_rows = jnp.sum(own, axis=1, keepdims=True) < EMPTY_SCORE
    best = jnp.max(jnp.where(first & (i != j), scores, -1.0), axis=1, keepdims=True)
    across = jnp.max(jnp.where(last_rows, scores[split:], -1.0), axis=0, keepdims=True)
    turned = [
        jnp.max(jnp.where(rows == lanes, across[:, k * DEVICES : (k + 1) * DEVICES], -1.0), axis=1, keepdims=True)
        for k in range(2)
    ]
    inside = jnp.max(jnp.where(last & (rows != lanes), corner, -1.0), axis=1, keepdims=True)
    best = jnp.maximum(best, jnp.concatenate([*turned, inside], axis=0))
    by_place = jnp.where(
        lanes == 0, best[:DEVICES], jnp.where(lanes == 1, best[DEVICES : 2 * DEVICES], best[2 * DEVICES :])
    )
    highest[...] = by_place.reshape(DEVICES, 1, 128)
    returned[0] = by_place[DEVICES - 1 :]

    for o in sorted(ORDER[:-1], key=distance, reverse=True):
        pltpu.make_async_remote_copy(
            src_ref=highest.at[ORDER.index(o)],
            dst_ref=returned.at[code(o)],
            send_sem=back_send_sem,
            recv_sem=back_recv_sem,
            device_id=around.back(o),
            device_id_type=MESH,
        ).start()

    back = returned.at[pl.ds(1, DEVICES - 1)]
    pltpu.make_async_copy(back, back, back_recv_sem).wait()

    mine = jnp.dot(
        named.astype(jnp.float32),
        returned[...].reshape(DEVICES, 128),
        precision=lax.Precision.HIGHEST,
        preferred_element_type=jnp.float32,
    )
    column = jnp.sum(jnp.where(lanes == place.astype(jnp.int32), mine, 0.0), axis=1, keepdims=True)
    out_ref[...] = jnp.sum(jnp.where(rows == lanes, column, 0.0), axis=0, keepdims=True)

    sent = outgoing.at[pl.ds(0, DEVICES - 1)]
    pltpu.make_async_copy(sent, sent, send_sem).wait()
    pltpu.make_async_copy(back, back, back_send_sem).wait()


def body(embeddings, cluster_ids):
    hbm = pl.BlockSpec(memory_space=pltpu.HBM)
    out = pl.pallas_call(
        kernel,
        out_shape=jax.ShapeDtypeStruct((1, ROWS), jnp.float32),
        in_specs=[hbm, hbm],
        out_specs=pl.BlockSpec(memory_space=pltpu.VMEM),
        scratch_shapes=[
            pltpu.VMEM((1, ROWS), jnp.int32),
            pltpu.VMEM((ROWS, D), jnp.bfloat16),
            pltpu.VMEM((ROWS + 1, Q, W), jnp.bfloat16),
            pltpu.VMEM((DEVICES, CAP, Q, W), jnp.bfloat16),
            pltpu.VMEM((DEVICES, CAP, Q, W), jnp.bfloat16),
            pltpu.VMEM((CAP * DEVICES, D), jnp.bfloat16),
            pltpu.VMEM((8, 128), jnp.int32),
            pltpu.SMEM((8, 128), jnp.int32),
            pltpu.VMEM((DEVICES, 1, 128), jnp.float32),
            pltpu.VMEM((DEVICES, 1, 128), jnp.float32),
            pltpu.SemaphoreType.DMA,
            pltpu.SemaphoreType.DMA,
            pltpu.SemaphoreType.DMA,
            pltpu.SemaphoreType.DMA,
            pltpu.SemaphoreType.DMA((GROUPS,)),
            pltpu.SemaphoreType.DMA,
            pltpu.SemaphoreType.DMA,
            pltpu.SemaphoreType.REGULAR,
            pltpu.SemaphoreType.REGULAR,
        ],
        compiler_params=pltpu.CompilerParams(
            collective_id=0, has_side_effects=True, vmem_limit_bytes=40 * 1024 * 1024
        ),
    )(
        pltpu.with_memory_space_constraint(cluster_ids.reshape(1, ROWS), pltpu.HBM),
        pltpu.with_memory_space_constraint(embeddings, pltpu.HBM),
    )
    return out.reshape(ROWS)


def solution(mesh):
    return jax.shard_map(
        body,
        mesh=mesh,
        in_specs=(P(("doc", "clu"), None), P(("doc", "clu"), None)),
        out_specs=P(("doc", "clu")),
        check_vma=False,
    )
```

```python
import random

import jax
import jax.numpy as jnp
from jax import lax
from jax.experimental import pallas as pl
from jax.experimental.pallas import tpu as pltpu
from jax.sharding import PartitionSpec as P

MESH = pl.DeviceIdType.MESH
DEVICES = 128
ROWS = 128
CAP = 3
D = 4096
Q = 16
W = D // Q
GROUP = 16
GROUPS = DEVICES // GROUP
EMPTY = 1.0
EMPTY_SCORE = 2.0


def axes(o):
    return sum(k != 0 for k in o[:3])


def distance(o):
    return sum(min(k, 4 - k) for k in o[:3])


def turn(o):
    return (4, 0, 1 if distance(o) > 2 else 3, 2)[axes(o)]


def order():
    every = [(x, z, y, c) for x in range(4) for z in range(4) for y in range(4) for c in range(2)]
    random.Random(0).shuffle(every)
    left = sorted(every, key=lambda o: (turn(o), -o[3], -distance(o)))
    done = []
    while left:
        now = [o for o in left if turn(o) == turn(left[0])]

        def clash(o):
            return sum(
                w * sum(a == b and a != 0 for a, b in zip(o[:3], q[:3])) for w, q in zip((8, 4, 2, 1), reversed(done))
            )

        best = min(now, key=clash)
        left.remove(best)
        done.append(best)
    return done[:-2] + [(0, 0, 0, 1), (0, 0, 0, 0)]


ORDER = order()
TWO = [turn(o) for o in ORDER].index(1)
THREE = [turn(o) for o in ORDER].index(2)


def code(o):
    return ((o[0] * 4 + o[1]) * 4 + o[2]) * 2 + o[3]


def position():
    doc, clu = lax.axis_index("doc"), lax.axis_index("clu")
    return doc, clu // 8, (clu // 2) % 4, clu % 2


class Around:
    def __init__(self, me):
        x, z, y, c = me
        self.x = [(x + k) % 4 for k in range(4)]
        self.z = [((z + k) % 4) * 8 for k in range(4)]
        self.y = [((y + k) % 4) * 2 for k in range(4)]
        self.c = [c, 1 - c]

    def to(self, o):
        return self.x[o[0]], self.z[o[1]] + self.y[o[2]] + self.c[o[3]]

    def back(self, o):
        return self.to((-o[0] % 4, -o[1] % 4, -o[2] % 4, o[3]))


def code_of(cluster, me):
    x, z, y, c = me
    dx = ((cluster >> 5) + (4 - x)) & 3
    dz = ((cluster >> 3) + (4 - z)) & 3
    dy = ((cluster >> 1) + (4 - y)) & 3
    dc = (cluster + c) & 1
    return ((dx * 4 + dz) * 4 + dy) * 2 + dc


def kernel(
    ids_hbm, emb_hbm, out_ref,
    ids_ref, emb_ref, blocks, outgoing, incoming, members, index_v, index_s, highest, returned,
    ids_sem, emb_sem, index_sem, send_sem, recv_sem, back_send_sem, back_recv_sem, lines_known, planes_known,
):
    me = position()
    around = Around(me)
    barrier = pltpu.get_barrier_semaphore()

    ids_in = pltpu.make_async_copy(ids_hbm, ids_ref, ids_sem)
    ids_in.start()
    rows_in = pltpu.make_async_copy(emb_hbm, emb_ref, emb_sem)
    rows_in.start()

    lines = [o for o in ORDER[:-1] if axes(o) < 2]
    for o in lines:
        pl.semaphore_signal(barrier, inc=1, device_id=around.back(o), device_id_type=MESH)

    rows = lax.broadcasted_iota(jnp.int32, (ROWS, DEVICES), 0)
    lanes = lax.broadcasted_iota(jnp.int32, (ROWS, DEVICES), 1)
    ids_in.wait()
    codes = code_of(ids_ref[...], me)
    named = jnp.transpose(jnp.broadcast_to(codes, (DEVICES, ROWS))) == lanes
    earlier = jnp.dot(
        (lanes < rows).astype(jnp.bfloat16), named.astype(jnp.bfloat16), preferred_element_type=jnp.float32
    )
    place = jnp.sum(jnp.where(named, earlier, 0.0), axis=1, keepdims=True)
    for p in range(CAP):
        here = named & (earlier == p)
        row = ROWS + jnp.sum(jnp.where(here, rows - ROWS, 0), axis=0, keepdims=True)
        index_v[p : p + 1, :] = jnp.clip(row, 0, ROWS)
    to_scalars = pltpu.make_async_copy(index_v, index_s, index_sem)
    to_scalars.start()

    a = lax.broadcasted_iota(jnp.int32, (GROUP * Q, GROUP * Q), 0)
    b = lax.broadcasted_iota(jnp.int32, (GROUP * Q, GROUP * Q), 1)
    swap = ((a // Q == b % GROUP) & (a % Q == b // GROUP)).astype(jnp.bfloat16)

    blocks[ROWS] = jnp.full((Q, W), EMPTY, jnp.bfloat16)
    rows_in.wait()
    for g in range(ROWS // GROUP):
        values = emb_ref[pl.ds(g * GROUP, GROUP)].astype(jnp.float32)
        squares = jnp.sum(values * values, axis=1, keepdims=True)
        normed = (values * lax.rsqrt(squares + 1e-06)).astype(jnp.bfloat16)
        parts = jnp.concatenate([normed[:, q * W : (q + 1) * W] for q in range(Q)], axis=0)
        swapped = jnp.dot(swap, parts, preferred_element_type=jnp.float32).astype(jnp.bfloat16)
        blocks[pl.ds(g * GROUP, GROUP)] = swapped.reshape(GROUP, Q, W)

    to_scalars.wait()
    pl.semaphore_wait(barrier, len(lines))
    for k in range(1, 4):
        for peer in ((k, 0, 0, 0), (0, 0, k, 0)):
            pl.semaphore_signal(lines_known, inc=1, device_id=around.to(peer), device_id_type=MESH)
    for n, o in enumerate(ORDER[:-1]):
        if n == TWO:
            pl.semaphore_wait(lines_known, 6)
            for k in range(1, 4):
                pl.semaphore_signal(planes_known, inc=1, device_id=around.to((k, 0, 0, 0)), device_id_type=MESH)
        if n == THREE:
            pl.semaphore_wait(planes_known, 3)
        for p in range(CAP):
            outgoing[n, p] = blocks[index_s[p, code(o)]]
        pltpu.make_async_remote_copy(
            src_ref=outgoing.at[n],
            dst_ref=incoming.at[n],
            send_sem=send_sem,
            recv_sem=recv_sem.at[n // GROUP],
            device_id=around.to(o),
            device_id_type=MESH,
        ).start()

    for p in range(CAP):
        incoming[DEVICES - 1, p] = blocks[index_s[p, 0]]

    def arrive(g, count):
        arrived = incoming.at[pl.ds(g * GROUP, count)]
        pltpu.make_async_copy(arrived, arrived, recv_sem.at[g]).wait()
        for p in range(CAP):
            parts = incoming[pl.ds(g * GROUP, GROUP), p].reshape(GROUP * Q, W)
            swapped = jnp.dot(swap, parts, preferred_element_type=jnp.float32).astype(jnp.bfloat16)
            where = pl.ds(pl.multiple_of(p * DEVICES + g * GROUP, GROUP), GROUP)
            for q in range(Q):
                members[where, q * W : (q + 1) * W] = swapped[q * GROUP : (q + 1) * GROUP]

    @pl.loop(0, GROUPS - 1)
    def _(g):
        arrive(g, GROUP)

    arrive(GROUPS - 1, GROUP - 1)

    split = 2 * DEVICES
    places = CAP * DEVICES
    scores = lax.dot_general(
        members[...], members[:split], (((1,), (1,)), ((), ())), preferred_element_type=jnp.float32
    )
    corner = lax.dot_general(
        members[split:], members[split:], (((1,), (1,)), ((), ())), preferred_element_type=jnp.float32
    )
    i = lax.broadcasted_iota(jnp.int32, (places, split), 0)
    j = lax.broadcasted_iota(jnp.int32, (places, split), 1)
    first = jnp.sum(jnp.where(i == j, scores, 0.0), axis=0, keepdims=True) < EMPTY_SCORE
    own = jnp.where(rows == lanes, corner, 0.0)
    last = jnp.sum(own, axis=0, keepdims=True) < EMPTY_SCORE
    last_rows = jnp.sum(own, axis=1, keepdims=True) < EMPTY_SCORE
    best = jnp.max(jnp.where(first & (i != j), scores, -1.0), axis=1, keepdims=True)
    across = jnp.max(jnp.where(last_rows, scores[split:], -1.0), axis=0, keepdims=True)
    turned = [
        jnp.max(jnp.where(rows == lanes, across[:, k * DEVICES : (k + 1) * DEVICES], -1.0), axis=1, keepdims=True)
        for k in range(2)
    ]
    inside = jnp.max(jnp.where(last & (rows != lanes), corner, -1.0), axis=1, keepdims=True)
    best = jnp.maximum(best, jnp.concatenate([*turned, inside], axis=0))
    by_place = jnp.where(
        lanes == 0, best[:DEVICES], jnp.where(lanes == 1, best[DEVICES : 2 * DEVICES], best[2 * DEVICES :])
    )
    highest[...] = by_place.reshape(DEVICES, 1, 128)
    returned[0] = by_place[DEVICES - 1 :]

    for o in sorted(ORDER[:-1], key=distance, reverse=True):
        pltpu.make_async_remote_copy(
            src_ref=highest.at[ORDER.index(o)],
            dst_ref=returned.at[code(o)],
            send_sem=back_send_sem,
            recv_sem=back_recv_sem,
            device_id=around.back(o),
            device_id_type=MESH,
        ).start()

    back = returned.at[pl.ds(1, DEVICES - 1)]
    pltpu.make_async_copy(back, back, back_recv_sem).wait()

    picks = named.astype(jnp.bfloat16)
    left = returned[...].reshape(DEVICES, 128)
    mine = jnp.zeros((ROWS, 128), jnp.float32)
    for _ in range(3):
        part = left.astype(jnp.bfloat16)
        mine += jnp.dot(picks, part, preferred_element_type=jnp.float32)
        left = left - part.astype(jnp.float32)
    column = jnp.sum(jnp.where(lanes == place.astype(jnp.int32), mine, 0.0), axis=1, keepdims=True)
    out_ref[...] = jnp.sum(jnp.where(rows == lanes, column, 0.0), axis=0, keepdims=True)

    sent = outgoing.at[pl.ds(0, DEVICES - 1)]
    pltpu.make_async_copy(sent, sent, send_sem).wait()
    pltpu.make_async_copy(back, back, back_send_sem).wait()


def body(embeddings, cluster_ids):
    hbm = pl.BlockSpec(memory_space=pltpu.HBM)
    out = pl.pallas_call(
        kernel,
        out_shape=jax.ShapeDtypeStruct((1, ROWS), jnp.float32),
        in_specs=[hbm, hbm],
        out_specs=pl.BlockSpec(memory_space=pltpu.VMEM),
        scratch_shapes=[
            pltpu.VMEM((1, ROWS), jnp.int32),
            pltpu.VMEM((ROWS, D), jnp.bfloat16),
            pltpu.VMEM((ROWS + 1, Q, W), jnp.bfloat16),
            pltpu.VMEM((DEVICES, CAP, Q, W), jnp.bfloat16),
            pltpu.VMEM((DEVICES, CAP, Q, W), jnp.bfloat16),
            pltpu.VMEM((CAP * DEVICES, D), jnp.bfloat16),
            pltpu.VMEM((8, 128), jnp.int32),
            pltpu.SMEM((8, 128), jnp.int32),
            pltpu.VMEM((DEVICES, 1, 128), jnp.float32),
            pltpu.VMEM((DEVICES, 1, 128), jnp.float32),
            pltpu.SemaphoreType.DMA,
            pltpu.SemaphoreType.DMA,
            pltpu.SemaphoreType.DMA,
            pltpu.SemaphoreType.DMA,
            pltpu.SemaphoreType.DMA((GROUPS,)),
            pltpu.SemaphoreType.DMA,
            pltpu.SemaphoreType.DMA,
            pltpu.SemaphoreType.REGULAR,
            pltpu.SemaphoreType.REGULAR,
        ],
        compiler_params=pltpu.CompilerParams(
            collective_id=0, has_side_effects=True, vmem_limit_bytes=40 * 1024 * 1024
        ),
    )(
        pltpu.with_memory_space_constraint(cluster_ids.reshape(1, ROWS), pltpu.HBM),
        pltpu.with_memory_space_constraint(embeddings, pltpu.HBM),
    )
    return out.reshape(ROWS)


def solution(mesh):
    return jax.shard_map(
        body,
        mesh=mesh,
        in_specs=(P(("doc", "clu"), None), P(("doc", "clu"), None)),
        out_specs=P(("doc", "clu")),
        check_vma=False,
    )
```

```python
import random

import jax
import jax.numpy as jnp
from jax import lax
from jax.experimental import pallas as pl
from jax.experimental.pallas import tpu as pltpu
from jax.sharding import PartitionSpec as P

MESH = pl.DeviceIdType.MESH
DEVICES = 128
ROWS = 128
CAP = 3
D = 4096
Q = 16
W = D // Q
GROUP = 16
GROUPS = DEVICES // GROUP
EMPTY = 1.0
EMPTY_SCORE = 2.0


def axes(o):
    return sum(k != 0 for k in o[:3])


def distance(o):
    return sum(min(k, 4 - k) for k in o[:3])


def turn(o):
    return (4, 0, 1 if distance(o) > 2 else 3, 2)[axes(o)]


def order():
    every = [(x, z, y, c) for x in range(4) for z in range(4) for y in range(4) for c in range(2)]
    random.Random(0).shuffle(every)
    left = sorted(every, key=lambda o: (turn(o), -o[3], -distance(o)))
    done = []
    while left:
        now = [o for o in left if turn(o) == turn(left[0])]

        def clash(o):
            return sum(
                w * sum(a == b and a != 0 for a, b in zip(o[:3], q[:3])) for w, q in zip((8, 4, 2, 1), reversed(done))
            )

        best = min(now, key=clash)
        left.remove(best)
        done.append(best)
    return done[:-2] + [(0, 0, 0, 1), (0, 0, 0, 0)]


ORDER = order()
TWO = [turn(o) for o in ORDER].index(1)
THREE = [turn(o) for o in ORDER].index(2)


def code(o):
    return ((o[0] * 4 + o[1]) * 4 + o[2]) * 2 + o[3]


def position():
    doc, clu = lax.axis_index("doc"), lax.axis_index("clu")
    return doc, clu // 8, (clu // 2) % 4, clu % 2


class Around:
    def __init__(self, me):
        x, z, y, c = me
        self.x = [(x + k) % 4 for k in range(4)]
        self.z = [((z + k) % 4) * 8 for k in range(4)]
        self.y = [((y + k) % 4) * 2 for k in range(4)]
        self.c = [c, 1 - c]

    def to(self, o):
        return self.x[o[0]], self.z[o[1]] + self.y[o[2]] + self.c[o[3]]

    def back(self, o):
        return self.to((-o[0] % 4, -o[1] % 4, -o[2] % 4, o[3]))


def code_of(cluster, me):
    x, z, y, c = me
    dx = ((cluster >> 5) + (4 - x)) & 3
    dz = ((cluster >> 3) + (4 - z)) & 3
    dy = ((cluster >> 1) + (4 - y)) & 3
    dc = (cluster + c) & 1
    return ((dx * 4 + dz) * 4 + dy) * 2 + dc


def kernel(
    ids_hbm, emb_hbm, out_ref,
    ids_ref, emb_ref, blocks, outgoing, incoming, members, index_v, index_s, highest, returned,
    ids_sem, emb_sem, index_sem, send_sem, recv_sem, back_send_sem, back_recv_sem, lines_known, planes_known,
):
    me = position()
    around = Around(me)
    barrier = pltpu.get_barrier_semaphore()

    ids_in = pltpu.make_async_copy(ids_hbm, ids_ref, ids_sem)
    ids_in.start()
    rows_in = pltpu.make_async_copy(emb_hbm, emb_ref, emb_sem)
    rows_in.start()

    lines = [o for o in ORDER[:-1] if axes(o) < 2]
    for o in lines:
        pl.semaphore_signal(barrier, inc=1, device_id=around.back(o), device_id_type=MESH)

    rows = lax.broadcasted_iota(jnp.int32, (ROWS, DEVICES), 0)
    lanes = lax.broadcasted_iota(jnp.int32, (ROWS, DEVICES), 1)
    ids_in.wait()
    codes = code_of(ids_ref[...], me)
    named = jnp.transpose(jnp.broadcast_to(codes, (DEVICES, ROWS))) == lanes
    earlier = jnp.dot(
        (lanes < rows).astype(jnp.bfloat16), named.astype(jnp.bfloat16), preferred_element_type=jnp.float32
    )
    place = jnp.sum(jnp.where(named, earlier, 0.0), axis=1, keepdims=True)
    for p in range(CAP):
        here = named & (earlier == p)
        row = ROWS + jnp.sum(jnp.where(here, rows - ROWS, 0), axis=0, keepdims=True)
        index_v[p : p + 1, :] = jnp.clip(row, 0, ROWS)
    to_scalars = pltpu.make_async_copy(index_v, index_s, index_sem)
    to_scalars.start()

    a = lax.broadcasted_iota(jnp.int32, (GROUP * Q, GROUP * Q), 0)
    b = lax.broadcasted_iota(jnp.int32, (GROUP * Q, GROUP * Q), 1)
    swap = ((a // Q == b % GROUP) & (a % Q == b // GROUP)).astype(jnp.bfloat16)

    blocks[ROWS] = jnp.full((Q, W), EMPTY, jnp.bfloat16)
    rows_in.wait()
    for g in range(ROWS // GROUP):
        values = emb_ref[pl.ds(g * GROUP, GROUP)].astype(jnp.float32)
        squares = jnp.sum(values * values, axis=1, keepdims=True)
        normed = (values * lax.rsqrt(squares + 1e-06)).astype(jnp.bfloat16)
        parts = jnp.concatenate([normed[:, q * W : (q + 1) * W] for q in range(Q)], axis=0)
        swapped = jnp.dot(swap, parts, preferred_element_type=jnp.float32).astype(jnp.bfloat16)
        blocks[pl.ds(g * GROUP, GROUP)] = swapped.reshape(GROUP, Q, W)

    to_scalars.wait()
    pl.semaphore_wait(barrier, len(lines))
    for k in range(1, 4):
        for peer in ((k, 0, 0, 0), (0, 0, k, 0)):
            pl.semaphore_signal(lines_known, inc=1, device_id=around.to(peer), device_id_type=MESH)
    for n, o in enumerate(ORDER[:-1]):
        if n == TWO:
            pl.semaphore_wait(lines_known, 6)
            for k in range(1, 4):
                pl.semaphore_signal(planes_known, inc=1, device_id=around.to((k, 0, 0, 0)), device_id_type=MESH)
        if n == THREE:
            pl.semaphore_wait(planes_known, 3)
        for p in range(CAP):
            outgoing[n, p] = blocks[index_s[p, code(o)]]
        for part in (pl.ds(0, 2), pl.ds(2, 1)):
            pltpu.make_async_remote_copy(
                src_ref=outgoing.at[n, part],
                dst_ref=incoming.at[n, part],
                send_sem=send_sem,
                recv_sem=recv_sem.at[n // GROUP],
                device_id=around.to(o),
                device_id_type=MESH,
            ).start()

    for p in range(CAP):
        incoming[DEVICES - 1, p] = blocks[index_s[p, 0]]

    def arrive(g, count):
        arrived = incoming.at[pl.ds(g * GROUP, count)]
        pltpu.make_async_copy(arrived, arrived, recv_sem.at[g]).wait()
        for p in range(CAP):
            parts = incoming[pl.ds(g * GROUP, GROUP), p].reshape(GROUP * Q, W)
            swapped = jnp.dot(swap, parts, preferred_element_type=jnp.float32).astype(jnp.bfloat16)
            where = pl.ds(pl.multiple_of(p * DEVICES + g * GROUP, GROUP), GROUP)
            for q in range(Q):
                members[where, q * W : (q + 1) * W] = swapped[q * GROUP : (q + 1) * GROUP]

    @pl.loop(0, GROUPS - 1)
    def _(g):
        arrive(g, GROUP)

    arrive(GROUPS - 1, GROUP - 1)

    split = 2 * DEVICES
    places = CAP * DEVICES
    scores = lax.dot_general(
        members[...], members[:split], (((1,), (1,)), ((), ())), preferred_element_type=jnp.float32
    )
    corner = lax.dot_general(
        members[split:], members[split:], (((1,), (1,)), ((), ())), preferred_element_type=jnp.float32
    )
    i = lax.broadcasted_iota(jnp.int32, (places, split), 0)
    j = lax.broadcasted_iota(jnp.int32, (places, split), 1)
    first = jnp.sum(jnp.where(i == j, scores, 0.0), axis=0, keepdims=True) < EMPTY_SCORE
    own = jnp.where(rows == lanes, corner, 0.0)
    last = jnp.sum(own, axis=0, keepdims=True) < EMPTY_SCORE
    last_rows = jnp.sum(own, axis=1, keepdims=True) < EMPTY_SCORE
    best = jnp.max(jnp.where(first & (i != j), scores, -1.0), axis=1, keepdims=True)
    across = jnp.max(jnp.where(last_rows, scores[split:], -1.0), axis=0, keepdims=True)
    turned = [
        jnp.max(jnp.where(rows == lanes, across[:, k * DEVICES : (k + 1) * DEVICES], -1.0), axis=1, keepdims=True)
        for k in range(2)
    ]
    inside = jnp.max(jnp.where(last & (rows != lanes), corner, -1.0), axis=1, keepdims=True)
    best = jnp.maximum(best, jnp.concatenate([*turned, inside], axis=0))
    by_place = jnp.where(
        lanes == 0, best[:DEVICES], jnp.where(lanes == 1, best[DEVICES : 2 * DEVICES], best[2 * DEVICES :])
    )
    highest[...] = by_place.reshape(DEVICES, 1, 128)
    returned[0] = by_place[DEVICES - 1 :]

    for o in sorted(ORDER[:-1], key=distance, reverse=True):
        pltpu.make_async_remote_copy(
            src_ref=highest.at[ORDER.index(o)],
            dst_ref=returned.at[code(o)],
            send_sem=back_send_sem,
            recv_sem=back_recv_sem,
            device_id=around.back(o),
            device_id_type=MESH,
        ).start()

    back = returned.at[pl.ds(1, DEVICES - 1)]
    pltpu.make_async_copy(back, back, back_recv_sem).wait()

    picks = named.astype(jnp.bfloat16)
    left = returned[...].reshape(DEVICES, 128)
    mine = jnp.zeros((ROWS, 128), jnp.float32)
    for _ in range(3):
        part = left.astype(jnp.bfloat16)
        mine += jnp.dot(picks, part, preferred_element_type=jnp.float32)
        left = left - part.astype(jnp.float32)
    column = jnp.sum(jnp.where(lanes == place.astype(jnp.int32), mine, 0.0), axis=1, keepdims=True)
    out_ref[...] = jnp.sum(jnp.where(rows == lanes, column, 0.0), axis=0, keepdims=True)

    sent = outgoing.at[pl.ds(0, DEVICES - 1)]
    pltpu.make_async_copy(sent, sent, send_sem).wait()
    pltpu.make_async_copy(back, back, back_send_sem).wait()


def body(embeddings, cluster_ids):
    hbm = pl.BlockSpec(memory_space=pltpu.HBM)
    out = pl.pallas_call(
        kernel,
        out_shape=jax.ShapeDtypeStruct((1, ROWS), jnp.float32),
        in_specs=[hbm, hbm],
        out_specs=pl.BlockSpec(memory_space=pltpu.VMEM),
        scratch_shapes=[
            pltpu.VMEM((1, ROWS), jnp.int32),
            pltpu.VMEM((ROWS, D), jnp.bfloat16),
            pltpu.VMEM((ROWS + 1, Q, W), jnp.bfloat16),
            pltpu.VMEM((DEVICES, CAP, Q, W), jnp.bfloat16),
            pltpu.VMEM((DEVICES, CAP, Q, W), jnp.bfloat16),
            pltpu.VMEM((CAP * DEVICES, D), jnp.bfloat16),
            pltpu.VMEM((8, 128), jnp.int32),
            pltpu.SMEM((8, 128), jnp.int32),
            pltpu.VMEM((DEVICES, 1, 128), jnp.float32),
            pltpu.VMEM((DEVICES, 1, 128), jnp.float32),
            pltpu.SemaphoreType.DMA,
            pltpu.SemaphoreType.DMA,
            pltpu.SemaphoreType.DMA,
            pltpu.SemaphoreType.DMA,
            pltpu.SemaphoreType.DMA((GROUPS,)),
            pltpu.SemaphoreType.DMA,
            pltpu.SemaphoreType.DMA,
            pltpu.SemaphoreType.REGULAR,
            pltpu.SemaphoreType.REGULAR,
        ],
        compiler_params=pltpu.CompilerParams(
            collective_id=0, has_side_effects=True, vmem_limit_bytes=40 * 1024 * 1024
        ),
    )(
        pltpu.with_memory_space_constraint(cluster_ids.reshape(1, ROWS), pltpu.HBM),
        pltpu.with_memory_space_constraint(embeddings, pltpu.HBM),
    )
    return out.reshape(ROWS)


def solution(mesh):
    return jax.shard_map(
        body,
        mesh=mesh,
        in_specs=(P(("doc", "clu"), None), P(("doc", "clu"), None)),
        out_specs=P(("doc", "clu")),
        check_vma=False,
    )
```
